32 devices in a mesh: groups: 2 (over y), pass: 4 (over z), cent: 2 (over x), rep: 2 (over core).
Axes of the slice: x: 2, y: 2, z: 4, core: 2. Of those that a mesh axis runs over, the one named last changes fastest.
Arguments:
- queries: bfloat16 [32, 32, 128], P(('groups', 'pass', 'cent', 'rep')), parts along dimension 0, may hold values from -6 to 6
- candidates: int32 [32, 64], P(('groups', 'pass', 'cent', 'rep')), parts along dimension 0, may hold values from 0 to 127, as said below
- residuals: bfloat16 [256, 128, 128], P(('groups', 'pass', 'cent')), parts along dimension 0, may hold values from -0.8984375 to 0.8984375
- centre_ids: int32 [256, 128], P(('groups', 'pass', 'cent')), parts along dimension 0, may hold values from 0 to 16383, as said below
- lengths: int32 [256], P(('groups', 'pass', 'cent')), parts along dimension 0, may hold values from 8 to 128
- centroids: bfloat16 [16384, 128], P(('pass', 'cent')), may hold values from -0.5 to 0.5
Outputs:
- centre_best: float32 [32, 32], P(('groups', 'pass', 'cent', 'rep')), parts along dimension 0
- scores: float32 [32, 64], P(('groups', 'pass', 'cent', 'rep')), parts along dimension 0
The draws below stay inside these ranges and needn't reach their ends.
There are 2 independent parts, one for each index of `groups`. The reference program is written for one: setup_inputs(seed, part) draws one part's arguments, and reference() takes and returns one part's arrays. A program takes and returns all parts, laid end to end along the dimension named above; an argument that names none is the same for every part. Nothing has to cross between parts.
Inputs may be any that keep to these rules, and one draw needn't show every extreme that they name: `candidates`: passage p is held by index p // 16 of pass and cent. Among the candidate entries of the queries of one rep index, at most 192 name passages of one holder, and exactly 192 do for some holders. Entries of one query may repeat. `centre_ids`: centre c is held by index c // 2048 of pass and cent. The tokens of the passages of one holder name centres of each holder exactly 16 * 128 / 8 times.
All inputs are finite; a program needn't handle non-finite values.
Results may differ from the reference program's by a relative error of at most 0.00031.
Values may be sent and summed in bfloat16 or wider, within the bound.
A program may use at most 64 MiB of HBM per device.

```python
import math
import jax
import jax.numpy as jnp
from jax import lax

DIM = 128
QT = 32
LP = 128
KC = 64
CENT_DEV = 2048
Q_DEV = 1
PS = 16
NC = 16384
NQ = 16
NP = 128
N_PASS = 4
N_CENT = 2
N_REP = 2


def draw_candidates(key, part):
    key = jax.random.fold_in(key, 11)
    owners = N_PASS * N_CENT
    capacity = 3 * Q_DEV * KC
    hot_count = max(1, owners // 16)
    tickets = Q_DEV * owners * KC
    rest = owners - hot_count

    def one_half(half_key):
        keys = jax.random.split(half_key, 4)
        order = jax.random.permutation(keys[0], owners).astype(jnp.int32)
        ticket = jnp.arange(tickets, dtype=jnp.int32)
        hot_owner = order[jnp.minimum(ticket // capacity, hot_count - 1)]
        spill = ticket - hot_count * capacity + jax.random.randint(keys[1], (tickets,), 0, 2)
        cold_owner = order[hot_count + jnp.mod(spill, rest)]
        owner = jnp.where(ticket < hot_count * capacity, hot_owner, cold_owner)
        slot = jax.random.randint(keys[2], (tickets,), 0, PS)
        ids = owner * PS + slot
        ids = ids[jax.random.permutation(keys[3], tickets)]
        return ids.reshape(owners, Q_DEV, KC)
    halves = jax.vmap(one_half)(jax.random.split(key, N_REP))
    return jnp.transpose(halves, (1, 0, 2, 3)).reshape(owners * N_REP * Q_DEV, KC).astype(jnp.int32)


def draw_centre_ids(key, part):
    key = jax.random.fold_in(key, 23)
    owners = N_PASS * N_CENT
    count = PS * LP

    def one_holder(holder_key):
        keys = jax.random.split(holder_key, 2)
        target = jnp.mod(jnp.arange(count, dtype=jnp.int32), owners)
        target = target[jax.random.permutation(keys[0], count)]
        offset = jax.random.randint(keys[1], (count,), 0, CENT_DEV)
        return (target * CENT_DEV + offset).reshape(PS, LP)
    table = jax.vmap(one_holder)(jax.random.split(key, owners))
    return table.reshape(NP, LP).astype(jnp.int32)


def place_ends(drawn, key, least, largest):
    longest = drawn.shape.index(max(drawn.shape))
    spots = []
    for shift in (0, 1):
        where = [jax.random.randint(jax.random.fold_in(key, axis), (), 0, length) for axis, length in enumerate(drawn.shape)]
        where[longest] = (where[longest] + shift) % drawn.shape[longest]
        spots.append(tuple(where))
    return drawn.at[spots[0]].set(least).at[spots[1]].set(largest)


def steps_of(key, extent, cuts, smallest, high):
    def one(position, blocks):
        draws = jax.random.uniform(jax.random.fold_in(jax.random.fold_in(key, 6), position), (blocks,), jnp.float32, smallest / len(cuts), high / len(cuts))
        return jnp.repeat(jnp.exp(draws), extent[position] // blocks).reshape((-1,) + (1,) * (len(extent) - position - 1))

    factor_of = one(*cuts[0])
    for cut in cuts[1:]:
        factor_of = factor_of * one(*cut)
    return factor_of


def gaussian(rng, dims, deviation, limit, cuts=(), kind=jnp.bfloat16):
    factor_of = steps_of(rng, dims, cuts, -0.22, 0.18) if cuts else 1.0
    result = jax.random.normal(rng, dims, jnp.float32) * deviation * factor_of
    return jnp.minimum(jnp.maximum(result, -limit), limit).astype(kind)


def setup_inputs(seed: int = 0, part: int = 0) -> dict:
    arg_keys = jax.random.split(jax.random.key(seed), 7)
    part_splits = jax.random.split(jax.random.fold_in(arg_keys[6], part), 7)
    queries = gaussian(part_splits[0], (NQ, QT, DIM), 1.0, 6.0, ((0, 16),))
    candidates = draw_candidates(jax.random.fold_in(jax.random.fold_in(arg_keys[6], part), 71), part)
    residuals = gaussian(part_splits[2], (NP, LP, DIM), 0.15, 0.8984375, ((0, 8),))
    centre_ids = draw_centre_ids(jax.random.fold_in(jax.random.fold_in(arg_keys[6], part), 71), part)
    lengths = place_ends(jax.random.randint(part_splits[4], (NP,), max(1, LP // 16), LP + 1), jax.random.fold_in(part_splits[4], 1), max(1, LP // 16), LP).astype(jnp.int32)
    centroids = gaussian(arg_keys[5], (NC, DIM), DIM ** -0.5, 0.5, ((0, 8),))
    return dict(queries=queries, candidates=candidates, residuals=residuals, centre_ids=centre_ids, lengths=lengths, centroids=centroids)


def reference(queries, candidates, residuals, centre_ids, lengths, centroids):
    tokens = queries.reshape(-1, queries.shape[2])
    block = math.gcd(tokens.shape[0], 256)

    def centre_max(rows):
        return jnp.max(jnp.dot(rows, centroids.T, preferred_element_type=jnp.float32), axis=1)

    centre_best = lax.map(centre_max, tokens.reshape(-1, block, tokens.shape[1])).reshape(queries.shape[0], queries.shape[1])

    def one_query(item):
        query, chosen = item
        decoded = (centroids[centre_ids[chosen]].astype(jnp.float32) + residuals[chosen].astype(jnp.float32)).astype(jnp.bfloat16)
        sims = jnp.einsum("qd,kpd->kqp", query.astype(jnp.float32), decoded.astype(jnp.float32))
        live = jnp.arange(residuals.shape[1], dtype=jnp.int32)[None, :] < lengths[chosen][:, None]
        best = jnp.max(jnp.where(live[:, None, :], sims, -jnp.inf), axis=2)
        return jnp.sum(best, axis=1) / queries.shape[1]

    scores = lax.map(one_query, (queries, candidates))
    return centre_best, scores
```

```python
import functools
import math

import jax
import jax.numpy as jnp
from jax import lax
from jax.experimental import pallas as pl
from jax.experimental.pallas import tpu as pltpu
from jax.sharding import PartitionSpec as P

MESH = pl.DeviceIdType.MESH
NT = (((1,), (1,)), ((), ()))
F32 = jnp.float32
BF16 = jnp.bfloat16


def iota(shape, axis):
    return lax.broadcasted_iota(jnp.int32, shape, axis)


def ones_where(mask):
    return jnp.where(mask, 1.0, 0.0).astype(BF16)


def log2(n):
    return n.bit_length() - 1


def fused_kernel(
    holders, n_cent,
    q_ref, cand_ref, res_ref, ids_ref, len_ref, cent_ref,
    best_ref, score_ref,
    q_all, req_out, req_in, found, rows, stat_out, stat_in, slot_ref, pick, pair_max,
    q_send, q_recv, r_send, r_recv, f_send, f_recv, x_send, x_recv, s_send, s_recv,
):
    qt, dim = q_ref.shape
    held, slots = ids_ref.shape
    centres = cent_ref.shape[0]
    half = rows.shape[2]
    me = lax.axis_index("pass") * n_cent + lax.axis_index("cent")
    rep = lax.axis_index("rep")

    def at(step):
        h = lax.rem(me + step + holders, holders)
        return {"pass": lax.div(h, n_cent), "cent": lax.rem(h, n_cent)}

    other = {"rep": 1 - rep}
    far_first = sorted(range(1, holders), key=lambda k: -min(k, holders - k))

    barrier = pltpu.get_barrier_semaphore()
    for k in range(1, holders):
        pl.semaphore_signal(barrier, inc=1, device_id=at(k), device_id_type=MESH)
    pl.semaphore_signal(barrier, inc=1, device_id=other, device_id_type=MESH)

    ids = ids_ref[...]
    target = ((ids >> log2(centres)) - me) & (holders - 1)
    local_id = ids & (centres - 1)
    masks = [jnp.where(target == k, 1.0, 0.0) for k in range(holders)]
    mask = jnp.concatenate(masks, axis=0).astype(BF16)
    rows_of = holders * held
    before = ones_where(iota((slots, slots), 0) < iota((slots, slots), 1))
    in_row = jnp.dot(mask, before, preferred_element_type=F32)
    total = jnp.dot(mask, jnp.ones((slots, slots), BF16), preferred_element_type=F32)
    a, b = iota((rows_of, rows_of), 0), iota((rows_of, rows_of), 1)
    above = ones_where(((a >> log2(held)) == (b >> log2(held))) & (b < a))
    rank_all = in_row + jnp.dot(above, total.astype(BF16), preferred_element_type=F32)
    rank = jnp.zeros((held, slots), F32)
    for k in range(holders):
        rank = rank + masks[k] * rank_all[k * held : (k + 1) * held]
    slot_ref[...] = target.astype(F32) * (2.0 * half) + rank

    low = (local_id & 255).astype(F32)
    high = (local_id >> 8).astype(F32)
    shifted = rank - (rep * half).astype(F32)
    by_rank = iota((half, slots), 0).astype(F32)
    by_holder = iota((holders, slots), 0)
    asked = jnp.zeros((2 * holders, half), F32)
    for p in range(held):
        at_rank = ones_where(shifted[p : p + 1] == by_rank)
        named = target[p : p + 1] == by_holder
        parts = jnp.concatenate(
            [jnp.where(named, low[p : p + 1], 0.0), jnp.where(named, high[p : p + 1], 0.0)], axis=0
        ).astype(BF16)
        asked = asked + lax.dot_general(parts, at_rank, NT, preferred_element_type=F32)
    asked = (asked[:holders] + 256.0 * asked[holders:]).astype(jnp.int32)
    for k in range(1, holders):
        req_out[k] = jnp.broadcast_to(asked[k : k + 1], (8, half))
    req_in[0] = jnp.broadcast_to(asked[0:1], (8, half))
    q_all[0] = q_ref[...]
    stat_out[...] = jnp.zeros_like(stat_out)

    pl.semaphore_wait(barrier, holders)

    def remote(src, dst, send, recv, device):
        return pltpu.make_async_remote_copy(
            src_ref=src, dst_ref=dst, send_sem=send, recv_sem=recv,
            device_id=device, device_id_type=MESH,
        )

    def req_copy(k):
        return remote(req_out.at[k], req_in.at[k], r_send.at[k], r_recv.at[k], at(k))

    def q_copy(k):
        return remote(q_ref, q_all.at[k], q_send.at[k], q_recv.at[k], at(k))

    def row_copy(k):
        return remote(found.at[k], rows.at[k, rep], f_send.at[k], f_recv.at[k], at(-k))

    def swap_copy(k):
        return remote(rows.at[k, rep], rows.at[k, rep], x_send.at[k], x_recv.at[k], other)

    def swap_arrival(k):
        return remote(rows.at[k, rep], rows.at[k, 1 - rep], x_send.at[k], x_recv.at[k], other)

    def stat_copy(k):
        return remote(stat_out, stat_in.at[k], s_send.at[k], s_recv.at[k], at(-k))

    for k in far_first:
        req_copy(k).start()
    for k in far_first:
        q_copy(k).start()

    lanes = iota((half, 128), 1)

    def across(row):
        return jnp.transpose(jnp.broadcast_to(row, (half, half)))

    def chosen(row, width):
        spread = across(row)
        return jnp.concatenate(
            [ones_where(spread - j * 128.0 == lanes.astype(F32)) for j in range(width // 128)], axis=1
        )

    for k in far_first + [0]:
        if k:
            req_copy(k).wait_recv()
        hit = chosen(req_in[k][0:1].astype(F32), centres)
        got = jnp.dot(hit, cent_ref[...], preferred_element_type=F32).astype(BF16)
        if k:
            found[k] = got
            row_copy(k).start()
        else:
            rows[0, rep] = got
            swap_copy(0).start()

    for k in far_first:
        q_copy(k).wait_recv()
    tokens = q_all[...].reshape(holders * qt, dim)
    best = None
    for j in range(centres // 256):
        part = lax.dot_general(
            cent_ref[j * 256 : (j + 1) * 256], tokens, NT, preferred_element_type=F32
        )
        best = part if best is None else jnp.maximum(best, part)
    best = jnp.max(best, axis=0, keepdims=True)
    width = holders * qt
    own = (iota((holders, width), 1) >> log2(qt)) == iota((holders, width), 0)
    fold = jnp.where((iota((width, 128), 0) & (qt - 1)) == iota((width, 128), 1), 1.0, 0.0)
    stat_out[holders : 2 * holders] = jnp.dot(
        jnp.where(own, best, 0.0), fold, precision=lax.Precision.HIGHEST, preferred_element_type=F32
    )

    def choose(p, _):
        row = slot_ref[pl.ds(p, 1), :]
        pick[p] = chosen(row, 2 * half * holders)
        return 0

    lax.fori_loop(0, held, choose, 0)

    near_first = far_first[::-1]
    for k in near_first:
        row_copy(k).wait_recv()
        swap_copy(k).start()
    for k in [0] + near_first:
        swap_arrival(k).wait_recv()

    step = math.gcd(held, 4)
    centre_rows = rows[...].reshape(holders * 2 * half, dim)
    spot = iota((slots, width), 0)
    for g in range(held // step):
        group = pick[g * step : (g + 1) * step].reshape(step * slots, 2 * half * holders)
        fetched = jnp.dot(group, centre_rows, preferred_element_type=F32)
        residual = res_ref[g * step : (g + 1) * step].reshape(step * slots, dim).astype(F32)
        decoded = (fetched + residual).astype(BF16)
        sims = lax.dot_general(decoded, tokens, NT, preferred_element_type=F32)
        for i in range(step):
            p = g * step + i
            live = jnp.where(spot < len_ref[p], sims[i * slots : (i + 1) * slots], -jnp.inf)
            pair_max[p : p + 1] = jnp.max(live, axis=0, keepdims=True)
    seg = jnp.where(own, 1.0, 0.0)
    table = lax.dot_general(
        seg, pair_max[...], NT, precision=lax.Precision.HIGHEST, preferred_element_type=F32
    )
    stat_out[0:holders, 0:held] = table / qt

    for k in far_first:
        stat_copy(k).start()
    for k in far_first:
        stat_copy(k).wait_recv()

    picked = [stat_out[0:1, 0:held]] + [stat_in[k][k : k + 1, 0:held] for k in range(1, holders)]
    maxima = stat_out[holders : holders + 1]
    for k in range(1, holders):
        maxima = jnp.maximum(maxima, stat_in[k][holders + k : holders + k + 1])
    best_ref[...] = maxima[:, 0:qt]
    table = jnp.concatenate(picked, axis=0)
    cand = cand_ref[...]
    kc = cand.shape[1]
    where_p = jnp.where(iota((held, kc), 0) == (cand & (held - 1)), 1.0, 0.0)
    value = jnp.dot(table, where_p, precision=lax.Precision.HIGHEST, preferred_element_type=F32)
    holder = ((cand >> log2(held)) - me) & (holders - 1)
    score_ref[...] = jnp.sum(
        jnp.where(iota((holders, kc), 0) == holder, value, 0.0), axis=0, keepdims=True
    )

    for k in range(1, holders):
        req_copy(k).wait_send()
        q_copy(k).wait_send()
        row_copy(k).wait_send()
        stat_copy(k).wait_send()
    for k in range(holders):
        swap_copy(k).wait_send()


def fused(queries, candidates, residuals, centre_ids, lengths, centroids):
    q_dev, qt, dim = queries.shape
    holders = lax.axis_size(("pass", "cent"))
    held, slots = centre_ids.shape
    half = held * slots // holders // 2
    vmem = pl.BlockSpec(memory_space=pltpu.VMEM)
    dma = lambda: pltpu.SemaphoreType.DMA((holders,))
    return pl.pallas_call(
        functools.partial(fused_kernel, holders, lax.axis_size("cent")),
        out_shape=(
            jax.ShapeDtypeStruct((q_dev, qt), F32),
            jax.ShapeDtypeStruct((q_dev, candidates.shape[1]), F32),
        ),
        in_specs=[vmem, vmem, vmem, vmem, pl.BlockSpec(memory_space=pltpu.SMEM), vmem],
        out_specs=(vmem, vmem),
        scratch_shapes=[
            pltpu.VMEM((holders, qt, dim), BF16),
            pltpu.VMEM((holders, 8, half), jnp.int32),
            pltpu.VMEM((holders, 8, half), jnp.int32),
            pltpu.VMEM((holders, half, dim), BF16),
            pltpu.VMEM((holders, 2, half, dim), BF16),
            pltpu.VMEM((2 * holders, 128), F32),
            pltpu.VMEM((holders, 2 * holders, 128), F32),
            pltpu.VMEM((held, slots), F32),
            pltpu.VMEM((held, slots, 2 * half * holders), BF16),
            pltpu.VMEM((held, holders * qt), F32),
        ]
        + [dma() for _ in range(10)],
        compiler_params=pltpu.CompilerParams(
            collective_id=0, has_side_effects=True, vmem_limit_bytes=40 * 1024 * 1024
        ),
    )(queries.reshape(qt, dim), candidates, residuals, centre_ids, lengths, centroids)


def fits(queries, residuals, centroids, holders, reps):
    q_dev, qt, dim = queries.shape
    held, slots = residuals.shape[:2]
    powers = all(n & (n - 1) == 0 for n in (qt, held, holders, centroids.shape[0]))
    return (
        powers and q_dev == 1 and reps == 2 and dim == 128 and slots == 128 and holders == 8
        and held * slots == 256 * holders and centroids.shape[0] % 256 == 0
    )


def on_device_large(queries, candidates, residuals, centre_ids, lengths, centroids):
    q_dev, qt, dim = queries.shape
    kc = candidates.shape[1]
    held, slots = (residuals.shape[0], residuals.shape[1])
    centres_here = centroids.shape[0]
    holders = lax.axis_size(("pass", "cent"))
    me = lax.axis_index(("pass", "cent"))
    flat_ids = centre_ids.reshape(-1)
    target = flat_ids // centres_here
    order = jnp.argsort(target, stable=True)
    each = flat_ids.shape[0] // holders
    requests = flat_ids[order].reshape(holders, each)
    found = centroids[
        lax.all_to_all(requests, ("pass", "cent"), split_axis=0, concat_axis=0, tiled=True)
        - me * centres_here
    ]
    arrived = lax.all_to_all(found, ("pass", "cent"), split_axis=0, concat_axis=0, tiled=True)
    inverse = jnp.zeros_like(order).at[order].set(jnp.arange(order.shape[0], dtype=jnp.int32))
    fetched = arrived.reshape(-1, dim)[inverse].reshape(held, slots, dim)
    gathered, cand_all = (
        lax.all_gather(queries, ("pass", "cent"), axis=0, tiled=True),
        lax.all_gather(candidates, ("pass", "cent"), axis=0, tiled=True),
    )
    half = gathered.shape[0]
    tokens = gathered.reshape(-1, dim)
    block = math.gcd(tokens.shape[0], 1024)

    def centre_max(rows):
        return jnp.max(
            jnp.einsum("td,cd->tc", rows, centroids, preferred_element_type=jnp.float32), axis=1
        )

    local_max = lax.map(centre_max, tokens.reshape(-1, block, dim)).reshape(half, qt)
    flat = cand_all.reshape(-1) - me * held
    mine = (flat >= 0) & (flat < held)
    slot_of = jnp.cumsum(mine.astype(jnp.int32)) - 1
    capacity = 3 * q_dev * kc
    spot_of = jnp.where(mine, slot_of, capacity)
    entry = (
        jnp.zeros((capacity,), jnp.int32)
        .at[spot_of]
        .set(jnp.arange(flat.shape[0], dtype=jnp.int32), mode="drop")
    )
    valid = jnp.arange(capacity, dtype=jnp.int32) < jnp.sum(mine.astype(jnp.int32))
    query_row = entry // kc
    passage_row = jnp.clip(flat[entry], 0, held - 1)
    q_rows = gathered[query_row]
    decoded = (fetched.astype(jnp.float32) + residuals.astype(jnp.float32)).astype(jnp.bfloat16)
    p_rows = decoded[passage_row]
    sims = jnp.einsum("sqd,spd->sqp", q_rows, p_rows, preferred_element_type=jnp.float32)
    live = jnp.arange(slots, dtype=jnp.int32)[None, :] < lengths[passage_row][:, None]
    best = jnp.max(jnp.where(live[:, None, :], sims, -jnp.inf), axis=2)
    pair_value = jnp.where(valid, jnp.sum(best, axis=1) / qt, 0.0)
    spot = jnp.where(valid, entry, half * kc)
    term = (
        jnp.zeros((half * kc,), jnp.float32).at[spot].set(pair_value, mode="drop").reshape(half, kc)
    )
    maxima = lax.pmax(local_max, ("pass", "cent"))
    centre_best = lax.dynamic_slice_in_dim(maxima, me * q_dev, q_dev, 0)
    scores = lax.psum_scatter(term, ("pass", "cent"), scatter_dimension=0, tiled=True)
    return (centre_best, scores)


def on_device(queries, candidates, residuals, centre_ids, lengths, centroids):
    args = (queries, candidates, residuals, centre_ids, lengths, centroids)
    if fits(queries, residuals, centroids, lax.axis_size(("pass", "cent")), lax.axis_size("rep")):
        return fused(*args)
    return on_device_large(*args)


def solution(mesh):
    return jax.shard_map(
        on_device,
        mesh=mesh,
        in_specs=(
            P(("groups", "pass", "cent", "rep"), None, None),
            P(("groups", "pass", "cent", "rep"), None),
            P(("groups", "pass", "cent"), None, None),
            P(("groups", "pass", "cent"), None),
            P(("groups", "pass", "cent")),
            P(("pass", "cent"), None),
        ),
        out_specs=(
            P(("groups", "pass", "cent", "rep"), None),
            P(("groups", "pass", "cent", "rep"), None),
        ),
        check_vma=False,
    )
```

```python
import functools
import math

import jax
import jax.numpy as jnp
from jax import lax
from jax.experimental import pallas as pl
from jax.experimental.pallas import tpu as pltpu
from jax.sharding import PartitionSpec as P

MESH = pl.DeviceIdType.MESH
NT = (((1,), (1,)), ((), ()))
F32 = jnp.float32
BF16 = jnp.bfloat16


def iota(shape, axis):
    return lax.broadcasted_iota(jnp.int32, shape, axis)


def ones_where(mask):
    return jnp.where(mask, 1.0, 0.0).astype(BF16)


def log2(n):
    return n.bit_length() - 1


def fused_kernel(
    holders, n_cent,
    q_hbm, cand_hbm, res_hbm, ids_hbm, len_hbm, cent_hbm,
    best_ref, score_ref,
    cand_ref, res_ref, ids_ref, len_ref, cent_ref, in_sem,
    q_all, req_out, req_in, found, rows, stat_out, stat_in, slot_ref, later_ref, later_all, pick, pair_max, wide_cent,
    q_send, q_recv, r_send, r_recv, f_send, f_recv, x_send, x_recv, s_send, s_recv,
):
    qt, dim = q_hbm.shape
    held, slots = ids_ref.shape
    centres = cent_ref.shape[0]
    half = rows.shape[2]
    me = lax.axis_index("pass") * n_cent + lax.axis_index("cent")
    rep = lax.axis_index("rep")

    def at(step):
        h = lax.rem(me + step + holders, holders)
        return {"pass": lax.div(h, n_cent), "cent": lax.rem(h, n_cent)}

    other = {"rep": 1 - rep}
    far_first = sorted(range(1, holders), key=lambda k: -min(k, holders - k))

    loads = [
        pltpu.make_async_copy(src, dst, in_sem.at[i])
        for i, (src, dst) in enumerate(
            [
                (ids_hbm, ids_ref),
                (cent_hbm, cent_ref),
                (q_hbm, q_all.at[0]),
                (res_hbm, res_ref),
                (len_hbm, len_ref),
                (cand_hbm, cand_ref),
            ]
        )
    ]
    ids_load, cent_load, q_load, res_load, len_load, cand_load = loads
    for load in loads:
        load.start()

    barrier = pltpu.get_barrier_semaphore()
    for k in range(1, holders):
        pl.semaphore_signal(barrier, inc=1, device_id=at(k), device_id_type=MESH)
    pl.semaphore_signal(barrier, inc=1, device_id=other, device_id_type=MESH)

    ids_load.wait()
    ids = ids_ref[...]
    target = ((ids >> log2(centres)) - me) & (holders - 1)
    local_id = ids & (centres - 1)
    masks = [jnp.where(target == k, 1.0, 0.0) for k in range(holders)]
    mask = jnp.concatenate(masks, axis=0).astype(BF16)
    rows_of = holders * held
    before = ones_where(iota((slots, slots), 0) < iota((slots, slots), 1))
    in_row = jnp.dot(mask, before, preferred_element_type=F32)
    total = jnp.dot(mask, jnp.ones((slots, slots), BF16), preferred_element_type=F32)
    a, b = iota((rows_of, rows_of), 0), iota((rows_of, rows_of), 1)
    above = ones_where(((a >> log2(held)) == (b >> log2(held))) & (b < a))
    rank_all = in_row + jnp.dot(above, total.astype(BF16), preferred_element_type=F32)
    rank = jnp.zeros((held, slots), F32)
    for k in range(holders):
        rank = rank + masks[k] * rank_all[k * held : (k + 1) * held]
    later = jnp.where(rank >= half, 1.0, 0.0)
    slot_ref[...] = target.astype(F32) * (1.0 * half) + rank - later * half
    later_ref[...] = later

    low = (local_id & 255).astype(F32)
    high = (local_id >> 8).astype(F32)
    shifted = rank - (rep * half).astype(F32)
    by_rank = iota((half, slots), 0).astype(F32)
    by_holder = iota((holders, slots), 0)
    asked = jnp.zeros((2 * holders, half), F32)
    for p in range(held):
        at_rank = ones_where(shifted[p : p + 1] == by_rank)
        named = target[p : p + 1] == by_holder
        parts = jnp.concatenate(
            [jnp.where(named, low[p : p + 1], 0.0), jnp.where(named, high[p : p + 1], 0.0)], axis=0
        ).astype(BF16)
        asked = asked + lax.dot_general(parts, at_rank, NT, preferred_element_type=F32)
    asked = (asked[:holders] + 256.0 * asked[holders:]).astype(jnp.int32)
    for k in range(1, holders):
        req_out[k] = jnp.broadcast_to(asked[k : k + 1], (8, half))
    req_in[0] = jnp.broadcast_to(asked[0:1], (8, half))
    stat_out[...] = jnp.zeros_like(stat_out)

    pl.semaphore_wait(barrier, holders)

    def remote(src, dst, send, recv, device):
        return pltpu.make_async_remote_copy(
            src_ref=src, dst_ref=dst, send_sem=send, recv_sem=recv,
            device_id=device, device_id_type=MESH,
        )

    def req_copy(k):
        return remote(req_out.at[k], req_in.at[k], r_send.at[k], r_recv.at[k], at(k))

    def q_copy(k):
        return remote(q_hbm, q_all.at[k], q_send.at[k], q_recv.at[k], at(k))

    def row_copy(k):
        return remote(found.at[k], rows.at[k, rep], f_send.at[k], f_recv.at[k], at(-k))

    def swap_copy(k):
        return remote(rows.at[k, rep], rows.at[k, rep], x_send.at[k], x_recv.at[k], other)

    def swap_arrival(k):
        return remote(rows.at[k, rep], rows.at[k, 1 - rep], x_send.at[k], x_recv.at[k], other)

    def stat_copy(k):
        return remote(stat_out, stat_in.at[k], s_send.at[k], s_recv.at[k], at(-k))

    for k in far_first:
        req_copy(k).start()
    for k in far_first:
        q_copy(k).start()

    lanes = iota((half, 128), 1)

    def across(row):
        return jnp.transpose(jnp.broadcast_to(row, (half, half)))

    def chosen(row, width):
        spread = across(row)
        return jnp.concatenate(
            [ones_where(spread - j * 128.0 == lanes.astype(F32)) for j in range(width // 128)], axis=1
        )

    def choose(p, _):
        here = pl.ds(p * slots, slots)
        pick[here] = chosen(slot_ref[pl.ds(p, 1), :], half * holders)
        later_all[here] = across(later_ref[pl.ds(p, 1), :])
        return 0


    middle = centres // 2
    cent_load.wait()
    wide_cent[:, 0:dim] = cent_ref[0:middle]
    wide_cent[:, dim : 2 * dim] = cent_ref[middle:centres]

    for k in far_first + [0]:
        if k:
            req_copy(k).wait_recv()
        name = req_in[k][0:1]
        hit = chosen((name & (middle - 1)).astype(F32), middle)
        both = jnp.dot(hit, wide_cent[...], preferred_element_type=F32)
        upper = across((name >> log2(middle)).astype(F32)) > 0.5
        got = jnp.where(upper, both[:, dim:], both[:, :dim]).astype(BF16)
        if k:
            found[k] = got
            row_copy(k).start()
        else:
            rows[0, rep] = got
            swap_copy(0).start()

    for k in far_first:
        q_copy(k).wait_recv()
    q_load.wait()
    tokens = q_all[...].reshape(holders * qt, dim)
    best = None
    for j in range(centres // 256):
        part = lax.dot_general(
            cent_ref[j * 256 : (j + 1) * 256], tokens, NT, preferred_element_type=F32
        )
        best = part if best is None else jnp.maximum(best, part)
    best = jnp.max(best, axis=0, keepdims=True)
    width = holders * qt
    own = (iota((holders, width), 1) >> log2(qt)) == iota((holders, width), 0)
    fold = jnp.where((iota((width, 128), 0) & (qt - 1)) == iota((width, 128), 1), 1.0, 0.0)
    stat_out[holders : 2 * holders] = jnp.dot(
        jnp.where(own, best, 0.0), fold, precision=lax.Precision.HIGHEST, preferred_element_type=F32
    )

    lax.fori_loop(0, held, choose, 0)

    near_first = far_first[::-1]
    for k in near_first:
        row_copy(k).wait_recv()
        swap_copy(k).start()
    for k in [0] + near_first:
        swap_arrival(k).wait_recv()

    res_load.wait()
    len_load.wait()
    wide_rows = jnp.concatenate(
        [rows[:, i].reshape(holders * half, dim) for i in range(2)], axis=1
    )
    tile = held * slots
    spot = iota((slots, width), 0)
    for g in range(held * slots // tile):
        here = slice(g * tile, (g + 1) * tile)
        both = jnp.dot(pick[here], wide_rows, preferred_element_type=F32)
        fetched = jnp.where(later_all[here] > 0.5, both[:, dim:], both[:, :dim])
        first = g * tile // slots
        residual = res_ref[first : first + tile // slots].reshape(tile, dim).astype(F32)
        decoded = (fetched + residual).astype(BF16)
        sims = lax.dot_general(decoded, tokens, NT, preferred_element_type=F32)
        for i in range(tile // slots):
            p = first + i
            live = jnp.where(spot < len_ref[p], sims[i * slots : (i + 1) * slots], -jnp.inf)
            pair_max[p : p + 1] = jnp.max(live, axis=0, keepdims=True)
    seg = jnp.where(own, 1.0, 0.0)
    table = lax.dot_general(
        seg, pair_max[...], NT, precision=lax.Precision.HIGHEST, preferred_element_type=F32
    )
    stat_out[0:holders, 0:held] = table / qt

    for k in far_first:
        stat_copy(k).start()
    for k in far_first:
        stat_copy(k).wait_recv()

    picked = [stat_out[0:1, 0:held]] + [stat_in[k][k : k + 1, 0:held] for k in range(1, holders)]
    maxima = stat_out[holders : holders + 1]
    for k in range(1, holders):
        maxima = jnp.maximum(maxima, stat_in[k][holders + k : holders + k + 1])
    best_ref[...] = maxima[:, 0:qt]
    table = jnp.concatenate(picked, axis=0)
    cand_load.wait()
    cand = cand_ref[...]
    kc = cand.shape[1]
    where_p = jnp.where(iota((held, kc), 0) == (cand & (held - 1)), 1.0, 0.0)
    value = jnp.dot(table, where_p, precision=lax.Precision.HIGHEST, preferred_element_type=F32)
    holder = ((cand >> log2(held)) - me) & (holders - 1)
    score_ref[...] = jnp.sum(
        jnp.where(iota((holders, kc), 0) == holder, value, 0.0), axis=0, keepdims=True
    )

    for k in range(1, holders):
        req_copy(k).wait_send()
        q_copy(k).wait_send()
        row_copy(k).wait_send()
        stat_copy(k).wait_send()
    for k in range(holders):
        swap_copy(k).wait_send()


def fused(queries, candidates, residuals, centre_ids, lengths, centroids):
    q_dev, qt, dim = queries.shape
    holders = lax.axis_size(("pass", "cent"))
    held, slots = centre_ids.shape
    half = held * slots // holders // 2
    vmem = pl.BlockSpec(memory_space=pltpu.VMEM)
    hbm = pl.BlockSpec(memory_space=pltpu.HBM)
    dma = lambda: pltpu.SemaphoreType.DMA((holders,))
    return pl.pallas_call(
        functools.partial(fused_kernel, holders, lax.axis_size("cent")),
        out_shape=(
            jax.ShapeDtypeStruct((q_dev, qt), F32),
            jax.ShapeDtypeStruct((q_dev, candidates.shape[1]), F32),
        ),
        in_specs=[hbm] * 6,
        out_specs=(vmem, vmem),
        scratch_shapes=[
            pltpu.VMEM(candidates.shape, jnp.int32),
            pltpu.VMEM(residuals.shape, BF16),
            pltpu.VMEM(centre_ids.shape, jnp.int32),
            pltpu.SMEM(lengths.shape, jnp.int32),
            pltpu.VMEM(centroids.shape, BF16),
            pltpu.SemaphoreType.DMA((6,)),
            pltpu.VMEM((holders, qt, dim), BF16),
            pltpu.VMEM((holders, 8, half), jnp.int32),
            pltpu.VMEM((holders, 8, half), jnp.int32),
            pltpu.VMEM((holders, half, dim), BF16),
            pltpu.VMEM((holders, 2, half, dim), BF16),
            pltpu.VMEM((2 * holders, 128), F32),
            pltpu.VMEM((holders, 2 * holders, 128), F32),
            pltpu.VMEM((held, slots), F32),
            pltpu.VMEM((held, slots), F32),
            pltpu.VMEM((held * slots, dim), F32),
            pltpu.VMEM((held * slots, half * holders), BF16),
            pltpu.VMEM((held, holders * qt), F32),
            pltpu.VMEM((centroids.shape[0] // 2, 2 * dim), BF16),
        ]
        + [dma() for _ in range(10)],
        compiler_params=pltpu.CompilerParams(
            collective_id=0, has_side_effects=True, vmem_limit_bytes=60 * 1024 * 1024
        ),
    )(queries.reshape(qt, dim), candidates, residuals, centre_ids, lengths, centroids)


def fits(queries, residuals, centroids, holders, reps):
    q_dev, qt, dim = queries.shape
    held, slots = residuals.shape[:2]
    powers = all(n & (n - 1) == 0 for n in (qt, held, holders, centroids.shape[0]))
    return (
        powers and q_dev == 1 and reps == 2 and dim == 128 and slots == 128 and holders == 8
        and held * slots == 256 * holders and centroids.shape[0] % 256 == 0
    )


def on_device_large(queries, candidates, residuals, centre_ids, lengths, centroids):
    q_dev, qt, dim = queries.shape
    kc = candidates.shape[1]
    held, slots = (residuals.shape[0], residuals.shape[1])
    centres_here = centroids.shape[0]
    holders = lax.axis_size(("pass", "cent"))
    me = lax.axis_index(("pass", "cent"))
    flat_ids = centre_ids.reshape(-1)
    target = flat_ids // centres_here
    order = jnp.argsort(target, stable=True)
    each = flat_ids.shape[0] // holders
    requests = flat_ids[order].reshape(holders, each)
    found = centroids[
        lax.all_to_all(requests, ("pass", "cent"), split_axis=0, concat_axis=0, tiled=True)
        - me * centres_here
    ]
    arrived = lax.all_to_all(found, ("pass", "cent"), split_axis=0, concat_axis=0, tiled=True)
    inverse = jnp.zeros_like(order).at[order].set(jnp.arange(order.shape[0], dtype=jnp.int32))
    fetched = arrived.reshape(-1, dim)[inverse].reshape(held, slots, dim)
    gathered, cand_all = (
        lax.all_gather(queries, ("pass", "cent"), axis=0, tiled=True),
        lax.all_gather(candidates, ("pass", "cent"), axis=0, tiled=True),
    )
    half = gathered.shape[0]
    tokens = gathered.reshape(-1, dim)
    block = math.gcd(tokens.shape[0], 1024)

    def centre_max(rows):
        return jnp.max(
            jnp.einsum("td,cd->tc", rows, centroids, preferred_element_type=jnp.float32), axis=1
        )

    local_max = lax.map(centre_max, tokens.reshape(-1, block, dim)).reshape(half, qt)
    flat = cand_all.reshape(-1) - me * held
    mine = (flat >= 0) & (flat < held)
    slot_of = jnp.cumsum(mine.astype(jnp.int32)) - 1
    capacity = 3 * q_dev * kc
    spot_of = jnp.where(mine, slot_of, capacity)
    entry = (
        jnp.zeros((capacity,), jnp.int32)
        .at[spot_of]
        .set(jnp.arange(flat.shape[0], dtype=jnp.int32), mode="drop")
    )
    valid = jnp.arange(capacity, dtype=jnp.int32) < jnp.sum(mine.astype(jnp.int32))
    query_row = entry // kc
    passage_row = jnp.clip(flat[entry], 0, held - 1)
    q_rows = gathered[query_row]
    decoded = (fetched.astype(jnp.float32) + residuals.astype(jnp.float32)).astype(jnp.bfloat16)
    p_rows = decoded[passage_row]
    sims = jnp.einsum("sqd,spd->sqp", q_rows, p_rows, preferred_element_type=jnp.float32)
    live = jnp.arange(slots, dtype=jnp.int32)[None, :] < lengths[passage_row][:, None]
    best = jnp.max(jnp.where(live[:, None, :], sims, -jnp.inf), axis=2)
    pair_value = jnp.where(valid, jnp.sum(best, axis=1) / qt, 0.0)
    spot = jnp.where(valid, entry, half * kc)
    term = (
        jnp.zeros((half * kc,), jnp.float32).at[spot].set(pair_value, mode="drop").reshape(half, kc)
    )
    maxima = lax.pmax(local_max, ("pass", "cent"))
    centre_best = lax.dynamic_slice_in_dim(maxima, me * q_dev, q_dev, 0)
    scores = lax.psum_scatter(term, ("pass", "cent"), scatter_dimension=0, tiled=True)
    return (centre_best, scores)


def on_device(queries, candidates, residuals, centre_ids, lengths, centroids):
    args = (queries, candidates, residuals, centre_ids, lengths, centroids)
    if fits(queries, residuals, centroids, lax.axis_size(("pass", "cent")), lax.axis_size("rep")):
        return fused(*args)
    return on_device_large(*args)


def solution(mesh):
    return jax.shard_map(
        on_device,
        mesh=mesh,
        in_specs=(
            P(("groups", "pass", "cent", "rep"), None, None),
            P(("groups", "pass", "cent", "rep"), None),
            P(("groups", "pass", "cent"), None, None),
            P(("groups", "pass", "cent"), None),
            P(("groups", "pass", "cent")),
            P(("pass", "cent"), None),
        ),
        out_specs=(
            P(("groups", "pass", "cent", "rep"), None),
            P(("groups", "pass", "cent", "rep"), None),
        ),
        check_vma=False,
    )
```

```python
import functools
import math

import jax
import jax.numpy as jnp
from jax import lax
from jax.experimental import pallas as pl
from jax.experimental.pallas import tpu as pltpu
from jax.sharding import PartitionSpec as P

MESH = pl.DeviceIdType.MESH
NT = (((1,), (1,)), ((), ()))
F32 = jnp.float32
BF16 = jnp.bfloat16


def iota(shape, axis):
    return lax.broadcasted_iota(jnp.int32, shape, axis)


def ones_where(mask):
    return jnp.where(mask, 1.0, 0.0).astype(BF16)


def log2(n):
    return n.bit_length() - 1


def fused_kernel(
    holders, n_cent,
    q_hbm, cand_hbm, res_hbm, ids_hbm, len_hbm, cent_hbm,
    out_ref,
    cand_ref, res_ref, ids_ref, len_ref, cent_ref, in_sem,
    q_all, req_out, req_in, found, rows, stat_out, stat_in, slot_ref, later_ref, later_all, pick, pair_max, wide_cent,
    q_send, q_recv, r_send, r_recv, f_send, f_recv, x_send, x_recv, s_send, s_recv,
):
    qt, dim = q_hbm.shape
    held, slots = ids_ref.shape
    centres = cent_ref.shape[0]
    half = rows.shape[2]
    me = lax.axis_index("pass") * n_cent + lax.axis_index("cent")
    rep = lax.axis_index("rep")

    def at(step):
        h = lax.rem(me + step + holders, holders)
        return {"pass": lax.div(h, n_cent), "cent": lax.rem(h, n_cent)}

    other = {"rep": 1 - rep}
    far_first = sorted(range(1, holders), key=lambda k: -min(k, holders - k))

    loads = [
        pltpu.make_async_copy(src, dst, in_sem.at[i])
        for i, (src, dst) in enumerate(
            [
                (ids_hbm, ids_ref),
                (cent_hbm, cent_ref),
                (q_hbm, q_all.at[0]),
                (res_hbm, res_ref),
                (len_hbm, len_ref),
                (cand_hbm, cand_ref),
            ]
        )
    ]
    ids_load, cent_load, q_load, res_load, len_load, cand_load = loads
    for load in loads:
        load.start()

    barrier = pltpu.get_barrier_semaphore()
    for k in range(1, holders):
        pl.semaphore_signal(barrier, inc=1, device_id=at(k), device_id_type=MESH)
    pl.semaphore_signal(barrier, inc=1, device_id=other, device_id_type=MESH)

    ids_load.wait()
    ids = ids_ref[...]
    target = ((ids >> log2(centres)) - me) & (holders - 1)
    local_id = ids & (centres - 1)
    masks = [jnp.where(target == k, 1.0, 0.0) for k in range(holders)]
    mask = jnp.concatenate(masks, axis=0).astype(BF16)
    rows_of = holders * held
    before = ones_where(iota((slots, slots), 0) < iota((slots, slots), 1))
    in_row = jnp.dot(mask, before, preferred_element_type=F32)
    total = jnp.dot(mask, jnp.ones((slots, slots), BF16), preferred_element_type=F32)
    a, b = iota((rows_of, rows_of), 0), iota((rows_of, rows_of), 1)
    above = ones_where(((a >> log2(held)) == (b >> log2(held))) & (b < a))
    rank_all = in_row + jnp.dot(above, total.astype(BF16), preferred_element_type=F32)
    rank = jnp.zeros((held, slots), F32)
    for k in range(holders):
        rank = rank + masks[k] * rank_all[k * held : (k + 1) * held]
    later = jnp.where(rank >= half, 1.0, 0.0)
    slot_ref[...] = target.astype(F32) * (1.0 * half) + rank - later * half
    later_ref[...] = later

    low = (local_id & 255).astype(F32)
    high = (local_id >> 8).astype(F32)
    shifted = rank - (rep * half).astype(F32)
    by_rank = iota((half, slots), 0).astype(F32)
    by_holder = iota((holders, slots), 0)
    asked = jnp.zeros((2 * holders, half), F32)
    for p in range(held):
        at_rank = ones_where(shifted[p : p + 1] == by_rank)
        named = target[p : p + 1] == by_holder
        parts = jnp.concatenate(
            [jnp.where(named, low[p : p + 1], 0.0), jnp.where(named, high[p : p + 1], 0.0)], axis=0
        ).astype(BF16)
        asked = asked + lax.dot_general(parts, at_rank, NT, preferred_element_type=F32)
    asked = (asked[:holders] + 256.0 * asked[holders:]).astype(jnp.int32)
    for k in range(1, holders):
        req_out[k] = jnp.broadcast_to(asked[k : k + 1], (8, half))
    req_in[0] = jnp.broadcast_to(asked[0:1], (8, half))
    stat_out[...] = jnp.zeros_like(stat_out)

    pl.semaphore_wait(barrier, holders)

    def remote(src, dst, send, recv, device):
        return pltpu.make_async_remote_copy(
            src_ref=src, dst_ref=dst, send_sem=send, recv_sem=recv,
            device_id=device, device_id_type=MESH,
        )

    def req_copy(k):
        return remote(req_out.at[k], req_in.at[k], r_send.at[k], r_recv.at[k], at(k))

    def q_copy(k):
        return remote(q_hbm, q_all.at[k], q_send.at[k], q_recv.at[k], at(k))

    def row_copy(k):
        return remote(found.at[k], rows.at[k, rep], f_send.at[k], f_recv.at[k], at(-k))

    def swap_copy(k):
        return remote(rows.at[k, rep], rows.at[k, rep], x_send.at[k], x_recv.at[k], other)

    def swap_arrival(k):
        return remote(rows.at[k, rep], rows.at[k, 1 - rep], x_send.at[k], x_recv.at[k], other)

    def stat_copy(k):
        return remote(stat_out, stat_in.at[k], s_send.at[k], s_recv.at[k], at(-k))

    for k in far_first:
        req_copy(k).start()
    for k in far_first:
        q_copy(k).start()

    lanes = iota((half, 128), 1)

    def across(row):
        return jnp.transpose(jnp.broadcast_to(row, (half, half)))

    def chosen(row, width):
        spread = across(row)
        return jnp.concatenate(
            [ones_where(spread - j * 128.0 == lanes.astype(F32)) for j in range(width // 128)], axis=1
        )

    def choose(p, _):
        here = pl.ds(p * slots, slots)
        pick[here] = chosen(slot_ref[pl.ds(p, 1), :], half * holders)
        later_all[here] = across(later_ref[pl.ds(p, 1), :])
        return 0


    lax.fori_loop(0, held // 2, choose, 0)

    middle = centres // 2
    cent_load.wait()
    wide_cent[:, 0:dim] = cent_ref[0:middle]
    wide_cent[:, dim : 2 * dim] = cent_ref[middle:centres]

    for k in far_first + [0]:
        if k:
            req_copy(k).wait_recv()
        name = req_in[k][0:1]
        hit = chosen((name & (middle - 1)).astype(F32), middle)
        both = jnp.dot(hit, wide_cent[...], preferred_element_type=F32)
        upper = across((name >> log2(middle)).astype(F32)) > 0.5
        got = jnp.where(upper, both[:, dim:], both[:, :dim]).astype(BF16)
        if k:
            found[k] = got
            row_copy(k).start()
        else:
            rows[0, rep] = got
            swap_copy(0).start()

    for k in far_first:
        q_copy(k).wait_recv()
    q_load.wait()
    tokens = q_all[...].reshape(holders * qt, dim)
    best = None
    for j in range(centres // 256):
        part = lax.dot_general(
            cent_ref[j * 256 : (j + 1) * 256], tokens, NT, preferred_element_type=F32
        )
        best = part if best is None else jnp.maximum(best, part)
    best = jnp.max(best, axis=0, keepdims=True)
    width = holders * qt
    own = (iota((holders, width), 1) >> log2(qt)) == iota((holders, width), 0)
    fold = jnp.where((iota((width, 128), 0) & (qt - 1)) == iota((width, 128), 1), 1.0, 0.0)
    stat_out[holders : 2 * holders] = jnp.dot(
        jnp.where(own, best, 0.0), fold, precision=lax.Precision.HIGHEST, preferred_element_type=F32
    )

    lax.fori_loop(held // 2, held, choose, 0)

    near_first = far_first[::-1]
    for k in near_first:
        row_copy(k).wait_recv()
        swap_copy(k).start()
    for k in [0] + near_first:
        swap_arrival(k).wait_recv()

    res_load.wait()
    len_load.wait()
    wide_rows = jnp.concatenate(
        [rows[:, i].reshape(holders * half, dim) for i in range(2)], axis=1
    )
    tile = held * slots
    spot = iota((slots, width), 0)
    for g in range(held * slots // tile):
        here = slice(g * tile, (g + 1) * tile)
        both = jnp.dot(pick[here], wide_rows, preferred_element_type=F32)
        fetched = jnp.where(later_all[here] > 0.5, both[:, dim:], both[:, :dim])
        first = g * tile // slots
        residual = res_ref[first : first + tile // slots].reshape(tile, dim).astype(F32)
        decoded = (fetched + residual).astype(BF16)
        sims = lax.dot_general(decoded, tokens, NT, preferred_element_type=F32)
        for i in range(tile // slots):
            p = first + i
            live = jnp.where(spot < len_ref[p], sims[i * slots : (i + 1) * slots], -jnp.inf)
            pair_max[p : p + 1] = jnp.max(live, axis=0, keepdims=True)
    seg = jnp.where(own, 1.0, 0.0)
    table = lax.dot_general(
        seg, pair_max[...], NT, precision=lax.Precision.HIGHEST, preferred_element_type=F32
    )
    stat_out[0:holders, 0:held] = table / qt

    for k in far_first:
        stat_copy(k).start()
    for k in far_first:
        stat_copy(k).wait_recv()

    picked = [stat_out[0:1, 0:held]] + [stat_in[k][k : k + 1, 0:held] for k in range(1, holders)]
    maxima = stat_out[holders : holders + 1]
    for k in range(1, holders):
        maxima = jnp.maximum(maxima, stat_in[k][holders + k : holders + k + 1])
    out_ref[:, 0:qt] = maxima[:, 0:qt]
    table = jnp.concatenate(picked, axis=0)
    cand_load.wait()
    cand = cand_ref[...]
    kc = cand.shape[1]
    where_p = jnp.where(iota((held, kc), 0) == (cand & (held - 1)), 1.0, 0.0)
    value = jnp.dot(table, where_p, precision=lax.Precision.HIGHEST, preferred_element_type=F32)
    holder = ((cand >> log2(held)) - me) & (holders - 1)
    out_ref[:, qt : qt + kc] = jnp.sum(
        jnp.where(iota((holders, kc), 0) == holder, value, 0.0), axis=0, keepdims=True
    )

    for k in range(1, holders):
        req_copy(k).wait_send()
        q_copy(k).wait_send()
        row_copy(k).wait_send()
        stat_copy(k).wait_send()
    for k in range(holders):
        swap_copy(k).wait_send()


def fused(queries, candidates, residuals, centre_ids, lengths, centroids):
    q_dev, qt, dim = queries.shape
    holders = lax.axis_size(("pass", "cent"))
    held, slots = centre_ids.shape
    half = held * slots // holders // 2
    vmem = pl.BlockSpec(memory_space=pltpu.VMEM)
    hbm = pl.BlockSpec(memory_space=pltpu.HBM)
    dma = lambda: pltpu.SemaphoreType.DMA((holders,))
    both = pl.pallas_call(
        functools.partial(fused_kernel, holders, lax.axis_size("cent")),
        out_shape=jax.ShapeDtypeStruct((q_dev, qt + candidates.shape[1]), F32),
        in_specs=[hbm] * 6,
        out_specs=vmem,
        scratch_shapes=[
            pltpu.VMEM(candidates.shape, jnp.int32),
            pltpu.VMEM(residuals.shape, BF16),
            pltpu.VMEM(centre_ids.shape, jnp.int32),
            pltpu.SMEM(lengths.shape, jnp.int32),
            pltpu.VMEM(centroids.shape, BF16),
            pltpu.SemaphoreType.DMA((6,)),
            pltpu.VMEM((holders, qt, dim), BF16),
            pltpu.VMEM((holders, 8, half), jnp.int32),
            pltpu.VMEM((holders, 8, half), jnp.int32),
            pltpu.VMEM((holders, half, dim), BF16),
            pltpu.VMEM((holders, 2, half, dim), BF16),
            pltpu.VMEM((2 * holders, 128), F32),
            pltpu.VMEM((holders, 2 * holders, 128), F32),
            pltpu.VMEM((held, slots), F32),
            pltpu.VMEM((held, slots), F32),
            pltpu.VMEM((held * slots, dim), F32),
            pltpu.VMEM((held * slots, half * holders), BF16),
            pltpu.VMEM((held, holders * qt), F32),
            pltpu.VMEM((centroids.shape[0] // 2, 2 * dim), BF16),
        ]
        + [dma() for _ in range(10)],
        compiler_params=pltpu.CompilerParams(
            collective_id=0, has_side_effects=True, vmem_limit_bytes=60 * 1024 * 1024
        ),
    )(queries.reshape(qt, dim), candidates, residuals, centre_ids, lengths, centroids)
    return both[:, :qt], both[:, qt:]


def fits(queries, residuals, centroids, holders, reps):
    q_dev, qt, dim = queries.shape
    held, slots = residuals.shape[:2]
    powers = all(n & (n - 1) == 0 for n in (qt, held, holders, centroids.shape[0]))
    return (
        powers and q_dev == 1 and reps == 2 and dim == 128 and slots == 128 and holders == 8
        and held * slots == 256 * holders and centroids.shape[0] % 256 == 0
    )


def on_device_large(queries, candidates, residuals, centre_ids, lengths, centroids):
    q_dev, qt, dim = queries.shape
    kc = candidates.shape[1]
    held, slots = (residuals.shape[0], residuals.shape[1])
    centres_here = centroids.shape[0]
    holders = lax.axis_size(("pass", "cent"))
    me = lax.axis_index(("pass", "cent"))
    flat_ids = centre_ids.reshape(-1)
    target = flat_ids // centres_here
    order = jnp.argsort(target, stable=True)
    each = flat_ids.shape[0] // holders
    requests = flat_ids[order].reshape(holders, each)
    found = centroids[
        lax.all_to_all(requests, ("pass", "cent"), split_axis=0, concat_axis=0, tiled=True)
        - me * centres_here
    ]
    arrived = lax.all_to_all(found, ("pass", "cent"), split_axis=0, concat_axis=0, tiled=True)
    inverse = jnp.zeros_like(order).at[order].set(jnp.arange(order.shape[0], dtype=jnp.int32))
    fetched = arrived.reshape(-1, dim)[inverse].reshape(held, slots, dim)
    gathered, cand_all = (
        lax.all_gather(queries, ("pass", "cent"), axis=0, tiled=True),
        lax.all_gather(candidates, ("pass", "cent"), axis=0, tiled=True),
    )
    half = gathered.shape[0]
    tokens = gathered.reshape(-1, dim)
    block = math.gcd(tokens.shape[0], 1024)

    def centre_max(rows):
        return jnp.max(
            jnp.einsum("td,cd->tc", rows, centroids, preferred_element_type=jnp.float32), axis=1
        )

    local_max = lax.map(centre_max, tokens.reshape(-1, block, dim)).reshape(half, qt)
    flat = cand_all.reshape(-1) - me * held
    mine = (flat >= 0) & (flat < held)
    slot_of = jnp.cumsum(mine.astype(jnp.int32)) - 1
    capacity = 3 * q_dev * kc
    spot_of = jnp.where(mine, slot_of, capacity)
    entry = (
        jnp.zeros((capacity,), jnp.int32)
        .at[spot_of]
        .set(jnp.arange(flat.shape[0], dtype=jnp.int32), mode="drop")
    )
    valid = jnp.arange(capacity, dtype=jnp.int32) < jnp.sum(mine.astype(jnp.int32))
    query_row = entry // kc
    passage_row = jnp.clip(flat[entry], 0, held - 1)
    q_rows = gathered[query_row]
    decoded = (fetched.astype(jnp.float32) + residuals.astype(jnp.float32)).astype(jnp.bfloat16)
    p_rows = decoded[passage_row]
    sims = jnp.einsum("sqd,spd->sqp", q_rows, p_rows, preferred_element_type=jnp.float32)
    live = jnp.arange(slots, dtype=jnp.int32)[None, :] < lengths[passage_row][:, None]
    best = jnp.max(jnp.where(live[:, None, :], sims, -jnp.inf), axis=2)
    pair_value = jnp.where(valid, jnp.sum(best, axis=1) / qt, 0.0)
    spot = jnp.where(valid, entry, half * kc)
    term = (
        jnp.zeros((half * kc,), jnp.float32).at[spot].set(pair_value, mode="drop").reshape(half, kc)
    )
    maxima = lax.pmax(local_max, ("pass", "cent"))
    centre_best = lax.dynamic_slice_in_dim(maxima, me * q_dev, q_dev, 0)
    scores = lax.psum_scatter(term, ("pass", "cent"), scatter_dimension=0, tiled=True)
    return (centre_best, scores)


def on_device(queries, candidates, residuals, centre_ids, lengths, centroids):
    args = (queries, candidates, residuals, centre_ids, lengths, centroids)
    if fits(queries, residuals, centroids, lax.axis_size(("pass", "cent")), lax.axis_size("rep")):
        return fused(*args)
    return on_device_large(*args)


def solution(mesh):
    return jax.shard_map(
        on_device,
        mesh=mesh,
        in_specs=(
            P(("groups", "pass", "cent", "rep"), None, None),
            P(("groups", "pass", "cent", "rep"), None),
            P(("groups", "pass", "cent"), None, None),
            P(("groups", "pass", "cent"), None),
            P(("groups", "pass", "cent")),
            P(("pass", "cent"), None),
        ),
        out_specs=(
            P(("groups", "pass", "cent", "rep"), None),
            P(("groups", "pass", "cent", "rep"), None),
        ),
        check_vma=False,
    )
```
